512 devices in a mesh: dp: 64 (over z_hi, x, y), group: 8 (over z_lo, core).
Axes of the slice: x: 4, y: 8, z: 8 (z_hi: 2, z_lo: 4; z = z_hi * 4 + z_lo), core: 2. Of those that a mesh axis runs over, the one named last changes fastest.
Arguments:
- sampled: bfloat16 [65536, 2304], P('dp', 'group'), may hold values from -6 to 6
- assignment: int32 [96], replicated, may hold values from 0 to 127, as said below
- inverse_rows: bfloat16 [128, 24, 2304], P('dp'), as said below
- gradient: bfloat16 [2304, 3072], P(None, 'group'), may hold values from -6 to 6
Outputs:
- factor_tiles: float32 [128, 24, 2304], P('dp', None, 'group')
- preconditioned: bfloat16 [2304, 3072], P(None, 'group')
The draws below stay inside these ranges and needn't reach their ends.
Inputs may be any that keep to these rules, and one draw needn't show every extreme that they name: assignment[t] is the slot holding tile t; slot s belongs to the owner at index s // 2 of dp; no two tiles share a slot; some owner holds 2 tiles. `inverse_rows`: slot assignment[t] holds the inverse factor's rows of tile t; slots that no tile names are not read.
All inputs are finite; a program needn't handle non-finite values.
Results may differ from the reference program's by a relative error of at most 0.0004.
Values may be sent and summed in bfloat16 or wider, within the bound.
No kernel may reach another device: no remote copies, remote signals or barrier semaphores. Data moves between devices by JAX's collectives and lax.ppermute only.
A program may use at most 64 MiB of HBM per device.

```python
import jax
import jax.numpy as jnp

BO = 2304
COLS = 3072
NTILES = 96
TILE = 24
CAP = 2
TOKENS = 65536
N_DP = 64


def slot_order(key):
    return jax.random.permutation(key, N_DP * CAP).astype(jnp.int32)


def draw_assignment(key, part):
    ordered = slot_order(key)
    return ordered[:NTILES]


def draw_inverse_rows(key, part):
    ordered = slot_order(key)
    position = jnp.argsort(ordered, stable=True).astype(jnp.int32)
    tile_of_slot = position % NTILES
    key = jax.random.fold_in(key, 7)
    noise_key, diag_key = jax.random.split(key)
    noise = jax.random.normal(noise_key, (N_DP * CAP, TILE, BO), jnp.float32)
    noise = noise * (1.0 / BO ** 0.5)
    diagonal = jax.random.uniform(diag_key, (N_DP * CAP, TILE, 1), jnp.float32, 1.0, 2.0)
    column_id = jnp.arange(BO, dtype=jnp.int32)[None, None, :]
    row_id = tile_of_slot[:, None, None] * TILE + jnp.arange(TILE, dtype=jnp.int32)[None, :, None]
    return (noise + jnp.where(column_id == row_id, diagonal, 0.0)).astype(jnp.bfloat16)


def steps_of(own_key, dims, pieces, smallest, top_value):
    gain = 1.0
    for dim, blocks in pieces:
        heights = jax.random.uniform(jax.random.fold_in(jax.random.fold_in(own_key, 6), dim), (blocks,), jnp.float32, smallest / len(pieces), top_value / len(pieces))
        gain = gain * jnp.repeat(jnp.exp(heights), dims[dim] // blocks).reshape((-1,) + (1,) * (len(dims) - 1 - dim))
    return gain


def centred(own_key, extent, width, reach, cuts=(), held_as=jnp.bfloat16):
    array = jax.random.normal(own_key, extent, jnp.float32) * width
    if len(cuts) > 0:
        array = steps_of(own_key, extent, cuts, -0.22, 0.18) * array
    return jnp.clip(array, min=-reach, max=reach).astype(held_as)


def setup_inputs(seed: int = 0) -> dict:
    key_list = jax.random.split(jax.random.key(seed), 5)
    sampled = centred(key_list[0], (TOKENS, BO), 1.0, 6.0, ((0, 64), (1, 8)))
    assignment = draw_assignment(jax.random.fold_in(key_list[4], 71), 0)
    inverse_rows = draw_inverse_rows(jax.random.fold_in(key_list[4], 71), 0)
    gradient = centred(key_list[3], (BO, COLS), 1.0, 6.0, ((1, 8),))
    return dict(sampled=sampled, assignment=assignment, inverse_rows=inverse_rows, gradient=gradient)


def reference(sampled, assignment, inverse_rows, gradient):
    total_rows = sampled.shape[0]
    gram_mean = jnp.dot(sampled.T, sampled, preferred_element_type=jnp.float32) * (1.0 / total_rows)
    gram_tiles = gram_mean.reshape(NTILES, TILE * BO)
    factor = jnp.zeros((N_DP * CAP, TILE * BO), jnp.float32).at[assignment].set(gram_tiles)
    factor_tiles = factor.reshape(N_DP * CAP, TILE, BO)
    full_inverse = jnp.take(inverse_rows, assignment, axis=0).reshape(BO, BO)
    preconditioned = jnp.dot(full_inverse, gradient, preferred_element_type=jnp.float32).astype(jnp.bfloat16)
    return factor_tiles, preconditioned
```

```python
import jax
import jax.numpy as jnp
from jax import lax
from jax.experimental import pallas as pl
from jax.experimental.pallas import tpu as pltpu
from jax.sharding import Mesh, PartitionSpec as P

DP = ("zh", "x", "yh", "yl")
GROUP = ("zl", "c")
NEAR = ("x", "yl")
FAR = ("yh", "zh")


def gram_kernel(tile_of, own_ref, all_ref, out_ref, rows_ref):
    tile = all_ref.shape[1]
    slots = out_ref.shape[2] // tile
    dest = pl.program_id(0)
    for pair in range(slots // 2):
        both = []
        for part in range(2):
            t = tile_of[dest * slots + 2 * pair + part]
            rows = all_ref[jnp.maximum(t, 0)].astype(jnp.float32)
            both.append(jnp.where(t >= 0, rows, 0.0))
        rows_ref[2 * tile * pair : 2 * tile * (pair + 1), :] = jnp.concatenate(both).astype(
            jnp.bfloat16
        )
    out_ref[0] = lax.dot_general(
        own_ref[...], rows_ref[...], (((1,), (1,)), ((), ())), preferred_element_type=jnp.float32
    )


def gram(tile_of, own, tiles, dests):
    count, tile, tokens = tiles.shape
    cols = own.shape[0]
    lanes = tile_of.shape[0] // dests * tile
    return pl.pallas_call(
        gram_kernel,
        grid_spec=pltpu.PrefetchScalarGridSpec(
            num_scalar_prefetch=1,
            grid=(dests,),
            in_specs=[
                pl.BlockSpec((cols, tokens), lambda d, t: (0, 0)),
                pl.BlockSpec((count, tile, tokens), lambda d, t: (0, 0, 0)),
            ],
            out_specs=pl.BlockSpec((1, cols, lanes), lambda d, t: (d, 0, 0)),
            scratch_shapes=[pltpu.VMEM((lanes, tokens), jnp.bfloat16)],
        ),
        out_shape=jax.ShapeDtypeStruct((dests, cols, lanes), jnp.float32),
        compiler_params=pltpu.CompilerParams(vmem_limit_bytes=48 * 2**20),
    )(tile_of, own, tiles)


def sum_turn_kernel(parts_ref, out_ref):
    total = parts_ref[0]
    for n in range(1, parts_ref.shape[0]):
        total = total + parts_ref[n]
    out_ref[...] = total.T


def sum_turn(parts):
    n, cols, lanes = parts.shape
    return pl.pallas_call(
        sum_turn_kernel,
        grid=(lanes // 128,),
        in_specs=[pl.BlockSpec((n, cols, 128), lambda i: (0, 0, i))],
        out_specs=pl.BlockSpec((128, cols), lambda i: (i, 0)),
        out_shape=jax.ShapeDtypeStruct((lanes, cols), jnp.float32),
        compiler_params=pltpu.CompilerParams(vmem_limit_bytes=32 * 2**20),
    )(parts)


def place_kernel(slot_of, rows_ref, out_ref):
    tile = rows_ref.shape[1]
    for pair in range(out_ref.shape[0] // (2 * tile)):
        both = [rows_ref[slot_of[2 * pair + n]].astype(jnp.float32) for n in range(2)]
        out_ref[2 * tile * pair : 2 * tile * (pair + 1), :] = jnp.concatenate(both).astype(
            out_ref.dtype
        )


def place(slot_of, rows):
    slots, tile, cols = rows.shape
    tiles = slot_of.shape[0]
    return pl.pallas_call(
        place_kernel,
        grid_spec=pltpu.PrefetchScalarGridSpec(
            num_scalar_prefetch=1,
            grid=(1,),
            in_specs=[pl.BlockSpec((slots, tile, cols), lambda i, s: (0, 0, 0))],
            out_specs=pl.BlockSpec((tiles * tile, cols), lambda i, s: (0, 0)),
        ),
        out_shape=jax.ShapeDtypeStruct((tiles * tile, cols), rows.dtype),
        compiler_params=pltpu.CompilerParams(vmem_limit_bytes=32 * 2**20),
    )(slot_of, rows)


def spread(rows, axis):
    copies = jnp.broadcast_to(rows[None], (lax.axis_size(axis),) + rows.shape)
    return lax.all_to_all(copies, axis, 0, 0)


def body(sampled, assignment, inverse_rows, gradient):
    n_zh, n_x, n_yh, n_yl = (lax.axis_size(name) for name in DP)
    held, tile, order = inverse_rows.shape
    tiles = assignment.shape[0]
    tokens, cols = sampled.shape
    width = gradient.shape[1]
    owners = n_zh * n_x * n_yh * n_yl

    own = sampled.T
    everything = lax.all_gather(own, GROUP, axis=0, tiled=True)

    mine = jnp.dot(
        inverse_rows.reshape(held * tile, order), gradient, preferred_element_type=jnp.float32
    ).astype(jnp.bfloat16)
    other = lax.ppermute(mine, "zh", [(0, 1), (1, 0)])
    first = lax.axis_index("zh") == 0
    rows = jnp.stack([jnp.where(first, mine, other), jnp.where(first, other, mine)])
    rows = spread(rows.reshape(n_zh * held * tile, width), ("yh", "yl"))
    rows = rows.reshape(n_yh * n_yl * n_zh * held * tile, width)
    rows = spread(rows, "x").reshape(owners * held, tile, width)
    place_of = jnp.arange(owners * held, dtype=jnp.int32).reshape(n_x, n_yh * n_yl, n_zh, held)
    slot_place = place_of.transpose(2, 0, 1, 3).reshape(-1)
    preconditioned = place(slot_place[assignment], rows)

    tile_of = (
        jnp.full((owners * held,), -1, jnp.int32)
        .at[assignment]
        .set(jnp.arange(tiles, dtype=jnp.int32))
    )
    tile_of = tile_of.reshape(n_zh, n_x, n_yh, n_yl, held).transpose(1, 3, 2, 0, 4).reshape(-1)
    near, far = n_x * n_yl, n_yh * n_zh
    scale = 1.0 / (tokens * owners)
    terms = gram(tile_of, own, everything.reshape(tiles, tile, tokens), near)
    terms = lax.all_to_all(terms, NEAR, 0, 0)
    terms = sum_turn(terms).reshape(far, held * tile, cols)
    terms = lax.all_to_all(terms, FAR, 0, 0)
    factor_tiles = (jnp.sum(terms, axis=0) * scale).reshape(held, tile, cols)
    return factor_tiles, preconditioned


def solution(mesh):
    split = Mesh(mesh.devices.reshape(2, 4, 4, 2, 4, 2), DP + GROUP)
    placed = (P(DP, GROUP), P(), P(DP, None, None), P(None, GROUP))
    return jax.shard_map(
        body,
        mesh=split,
        in_specs=placed,
        out_specs=(P(DP, None, GROUP), P(None, GROUP)),
        check_vma=False,
    )
```

```python
import functools

import jax
import jax.numpy as jnp
from jax import lax
from jax.experimental import pallas as pl
from jax.experimental.pallas import tpu as pltpu
from jax.sharding import Mesh, PartitionSpec as P

DP = ("zh", "x", "yh", "yl")
GROUP = ("zl", "c")
NEAR = ("x", "yl")
FAR = ("yh", "zh")


def gram_kernel(table, all_ref, keep_ref, send_ref, cols_ref, rows_ref):
    runs, _, tile, tokens = all_ref.shape
    half = keep_ref.shape[1]
    slots = keep_ref.shape[2] // tile
    count = pl.num_programs(0) * slots
    dest = pl.program_id(0)

    def fetch(to_ref, pair, places):
        for run in range(runs):
            both = []
            for place in places:
                rows = all_ref[run, jnp.maximum(place, 0)].astype(jnp.float32)
                both.append(jnp.where(place >= 0, rows, 0.0))
            to_ref[2 * tile * pair : 2 * tile * (pair + 1), tokens * run : tokens * (run + 1)] = (
                jnp.concatenate(both).astype(jnp.bfloat16)
            )

    @pl.when(dest == 0)
    def _():
        per = half // tile
        for core in range(2):
            for pair in range(per // 2):
                start = table[count + core] + 2 * pair
                fetch(cols_ref, core * per // 2 + pair, (start, start + 1))

    for pair in range(slots // 2):
        at = dest * slots + 2 * pair
        fetch(rows_ref, pair, (table[at], table[at + 1]))
    terms = lax.dot_general(
        cols_ref[...], rows_ref[...], (((1,), (1,)), ((), ())), preferred_element_type=jnp.float32
    )
    keep_ref[0] = terms[:half]
    send_ref[0] = terms[half:]


def gram(table, everything, dests, slots, half):
    runs, count, tile, tokens = everything.shape
    lanes = slots // dests * tile
    out = jax.ShapeDtypeStruct((dests, half, lanes), jnp.float32)
    return pl.pallas_call(
        gram_kernel,
        grid_spec=pltpu.PrefetchScalarGridSpec(
            num_scalar_prefetch=1,
            grid=(dests,),
            in_specs=[pl.BlockSpec((runs, count, tile, tokens), lambda d, t: (0, 0, 0, 0))],
            out_specs=[pl.BlockSpec((1, half, lanes), lambda d, t: (d, 0, 0))] * 2,
            scratch_shapes=[
                pltpu.VMEM((2 * half, runs * tokens), jnp.bfloat16),
                pltpu.VMEM((lanes, runs * tokens), jnp.bfloat16),
            ],
        ),
        out_shape=[out, out],
        compiler_params=pltpu.CompilerParams(vmem_limit_bytes=48 * 2**20),
    )(table, everything)


def sum_turn_kernel(parts_ref, out_ref):
    total = parts_ref[0]
    for n in range(1, parts_ref.shape[0]):
        total = total + parts_ref[n]
    total = total.T
    dests = out_ref.shape[0]
    rows, cols = total.shape[0] // dests, total.shape[1]
    for dest in range(dests):
        mine = total[rows * dest : rows * (dest + 1)]
        out_ref[dest, :rows] = mine[:, :128]
        rest = [mine[8 * n : 8 * n + 8, 128:] for n in range(rows // 8)]
        rest.append(jnp.zeros((8, 128 - (cols - 128) * (rows // 8)), jnp.float32))
        out_ref[dest, rows:] = jnp.concatenate(rest, axis=1)


def sum_turn(parts, dests):
    n, cols, lanes = parts.shape
    return pl.pallas_call(
        sum_turn_kernel,
        out_shape=jax.ShapeDtypeStruct((dests, lanes // dests + 8, 128), jnp.float32),
        compiler_params=pltpu.CompilerParams(vmem_limit_bytes=32 * 2**20),
    )(parts)


def sum_join_kernel(scale, parts_ref, out_ref):
    held, tile, cols = out_ref.shape
    halves, rows = parts_ref.shape[1], held * tile
    extra = cols // halves - 128
    pieces = []
    for half in range(halves):
        total = parts_ref[0, half]
        for n in range(1, parts_ref.shape[0]):
            total = total + parts_ref[n, half]
        total = total * scale
        pieces.append(total[:rows])
        rest = total[rows:]
        pieces.append(
            jnp.concatenate([rest[:, extra * n : extra * (n + 1)] for n in range(rows // 8)])
        )
    joined = jnp.concatenate(pieces, axis=1)
    for slot in range(held):
        out_ref[slot] = joined[tile * slot : tile * (slot + 1)]


def sum_join(parts, held, tile, cols, scale):
    return pl.pallas_call(
        functools.partial(sum_join_kernel, scale),
        out_shape=jax.ShapeDtypeStruct((held, tile, cols), jnp.float32),
    )(parts)


def place_kernel(slot_of, rows_ref, out_ref):
    tile = rows_ref.shape[1]
    for pair in range(out_ref.shape[0] // (2 * tile)):
        both = [rows_ref[slot_of[2 * pair + n]].astype(jnp.float32) for n in range(2)]
        out_ref[2 * tile * pair : 2 * tile * (pair + 1), :] = jnp.concatenate(both).astype(
            out_ref.dtype
        )


def place(slot_of, rows):
    slots, tile, cols = rows.shape
    tiles = slot_of.shape[0]
    return pl.pallas_call(
        place_kernel,
        grid_spec=pltpu.PrefetchScalarGridSpec(
            num_scalar_prefetch=1,
            grid=(1,),
            in_specs=[pl.BlockSpec((slots, tile, cols), lambda i, s: (0, 0, 0))],
            out_specs=pl.BlockSpec((tiles * tile, cols), lambda i, s: (0, 0)),
        ),
        out_shape=jax.ShapeDtypeStruct((tiles * tile, cols), rows.dtype),
        compiler_params=pltpu.CompilerParams(vmem_limit_bytes=32 * 2**20),
    )(slot_of, rows)


def spread(rows, axis):
    copies = jnp.broadcast_to(rows[None], (lax.axis_size(axis),) + rows.shape)
    return lax.all_to_all(copies, axis, 0, 0)


def body(sampled, assignment, inverse_rows, gradient):
    n_zh, n_x, n_yh, n_yl = (lax.axis_size(name) for name in DP)
    held, tile, order = inverse_rows.shape
    tiles = assignment.shape[0]
    tokens, cols = sampled.shape
    width = gradient.shape[1]
    owners = n_zh * n_x * n_yh * n_yl

    core, run = lax.axis_index("c"), lax.axis_index("zl")
    upper = lax.axis_index("zh")
    own = sampled.T
    kept = lax.dynamic_slice(own, (0, core * (tokens // 2)), (cols, tokens // 2))
    swapped = lax.dynamic_slice(own, (0, (1 - core) * (tokens // 2)), (cols, tokens // 2))
    swapped = lax.ppermute(swapped, "c", [(0, 1), (1, 0)])
    everything = lax.all_gather(jnp.concatenate([kept, swapped]), ("zh", "zl"), axis=0, tiled=True)

    mine = jnp.dot(
        inverse_rows.reshape(held * tile, order), gradient, preferred_element_type=jnp.float32
    ).astype(jnp.bfloat16)
    other = lax.ppermute(mine, "zh", [(0, 1), (1, 0)])
    first = lax.axis_index("zh") == 0
    rows = jnp.stack([jnp.where(first, mine, other), jnp.where(first, other, mine)])
    rows = spread(rows.reshape(n_zh * held * tile, width), ("yh", "yl"))
    rows = rows.reshape(n_yh * n_yl * n_zh * held * tile, width)
    rows = spread(rows, "x").reshape(owners * held, tile, width)
    everything, rows = lax.optimization_barrier((everything, rows))
    place_of = jnp.arange(owners * held, dtype=jnp.int32).reshape(n_x, n_yh * n_yl, n_zh, held)
    slot_place = place_of.transpose(2, 0, 1, 3).reshape(-1)
    preconditioned = place(slot_place[assignment], rows)

    near, far = n_x * n_yl, n_yh * n_zh
    per = cols // tile
    index = jnp.arange(tiles, dtype=jnp.int32)
    place_of = index // (2 * per) * (2 * per) + index % per
    place_of = place_of + jnp.where(index // per % 2 == core, 0, per)
    table = jnp.full((owners * held,), -1, jnp.int32).at[assignment].set(place_of)
    table = table.reshape(n_zh, n_x, n_yh, n_yl, held).transpose(1, 3, 2, 0, 4).reshape(-1)
    start = run * (2 * per) + upper * (per // n_zh)
    table = jnp.concatenate([table, jnp.stack([start, start + per]).astype(jnp.int32)])
    half = cols // n_zh
    keep, send = gram(
        table, everything.reshape(n_zh, tiles, tile, tokens // 2), near, owners * held, half
    )
    terms = keep + lax.ppermute(send, "c", [(0, 1), (1, 0)])
    terms = lax.all_to_all(terms, NEAR, 0, 0)
    terms = lax.all_to_all(sum_turn(terms, far), FAR, 0, 0)
    terms = terms.reshape((n_yh, n_zh) + terms.shape[1:])
    factor_tiles = sum_join(terms, held, tile, cols, 1.0 / (tokens * owners))
    return factor_tiles, preconditioned


def solution(mesh):
    split = Mesh(mesh.devices.reshape(2, 4, 4, 2, 4, 2), DP + GROUP)
    placed = (P(DP, GROUP), P(), P(DP, None, None), P(None, GROUP))
    return jax.shard_map(
        body,
        mesh=split,
        in_specs=placed,
        out_specs=(P(DP, None, GROUP), P(None, GROUP)),
        check_vma=False,
    )
```

```python
import functools

import jax
import jax.numpy as jnp
from jax import lax
from jax.experimental import pallas as pl
from jax.experimental.pallas import tpu as pltpu
from jax.sharding import Mesh, PartitionSpec as P

DP = ("zh", "x", "yh", "yl")
GROUP = ("zl", "c")
NEAR = ("x", "yl")
FAR = ("yh", "zh")


def gram_kernel(table, slots, own_ref, twin_ref, far_twin_ref, *refs):
    *others, keep_ref, send_ref, factors_ref, keep_sum, send_sum = refs
    blocks = [own_ref] + others
    far_ref = others[3]
    cols = own_ref.shape[0]
    share = keep_sum.shape[1]
    dest = pl.program_id(0)
    pairs = slots // 2
    tile = 24
    high = keep_ref.shape[1] // pairs
    count = pl.num_programs(0) * slots

    @pl.when(dest == 0)
    def _():
        start = pl.multiple_of(table[count], 16)
        mine = pl.ds(start, share)
        factors_ref[0, 0] = own_ref[mine, :]
        factors_ref[0, 1] = far_ref[mine, :]
        factors_ref[1, 0] = twin_ref[mine, :]
        factors_ref[1, 1] = far_twin_ref[mine, :]
        keep_sum[...] = jnp.zeros_like(keep_sum)
        send_sum[...] = jnp.zeros_like(send_sum)
        for n, block in enumerate(blocks):
            at = pl.ds(pl.multiple_of(table[count + 1 + 2 * n], 8), cols)
            which = table[count + 2 + 2 * n]
            for part, total in enumerate((keep_sum, send_sum)):
                total[at, :] += lax.dot_general(
                    block[...],
                    factors_ref[part, which],
                    (((1,), (1,)), ((), ())),
                    preferred_element_type=jnp.float32,
                )

    for total, out_ref in ((keep_sum, keep_ref), (send_sum, send_ref)):
        for pair in range(pairs):
            both = []
            for n in range(2):
                t = table[dest * slots + 2 * pair + n]
                rows = total[pl.ds(pl.multiple_of(jnp.maximum(t, 0) * tile, 8), tile), :]
                both.append(jnp.where(t >= 0, rows, 0.0))
            out_ref[0, high * pair : high * (pair + 1), :] = pack(jnp.concatenate(both))


def pack(rows):
    n, cols = rows.shape
    rest = [rows[8 * k : 8 * k + 8, 128:] for k in range(n // 8)]
    rest.append(jnp.zeros((8, 128 - (cols - 128) * (n // 8)), rows.dtype))
    return jnp.concatenate([rows[:, :128], jnp.concatenate(rest, axis=1)])


def gram(table, own, twin, far_twin, others, dests, slots, tile, share):
    cols, tokens = own.shape
    order = 8 * cols
    high = 2 * tile + 8
    out = jax.ShapeDtypeStruct((dests, slots // 2 * high, 128), jnp.float32)
    given = [own, twin, far_twin, *others]
    return pl.pallas_call(
        lambda table_ref, *refs: gram_kernel(table_ref, slots, *refs),
        grid_spec=pltpu.PrefetchScalarGridSpec(
            num_scalar_prefetch=1,
            grid=(dests,),
            in_specs=[pl.BlockSpec((cols, tokens), lambda d, t: (0, 0))] * len(given),
            out_specs=[pl.BlockSpec((1,) + out.shape[1:], lambda d, t: (d, 0, 0))] * 2,
            scratch_shapes=[
                pltpu.VMEM((2, 2, share, tokens), jnp.bfloat16),
                pltpu.VMEM((order, share), jnp.float32),
                pltpu.VMEM((order, share), jnp.float32),
            ],
        ),
        out_shape=[out, out],
        compiler_params=pltpu.CompilerParams(vmem_limit_bytes=56 * 2**20),
    )(table, *given)


def sum_join_kernel(scale, parts_ref, out_ref):
    held, tile, cols = out_ref.shape
    halves, rows = parts_ref.shape[1], held * tile
    extra = cols // halves - 128
    pieces = []
    for half in range(halves):
        total = parts_ref[0, half]
        for n in range(1, parts_ref.shape[0]):
            total = total + parts_ref[n, half]
        total = total * scale
        pieces.append(total[:rows])
        rest = total[rows:]
        pieces.append(
            jnp.concatenate([rest[:, extra * n : extra * (n + 1)] for n in range(rows // 8)])
        )
    joined = jnp.concatenate(pieces, axis=1)
    for slot in range(held):
        out_ref[slot] = joined[tile * slot : tile * (slot + 1)]


def sum_join(parts, held, tile, cols, scale):
    return pl.pallas_call(
        functools.partial(sum_join_kernel, scale),
        out_shape=jax.ShapeDtypeStruct((held, tile, cols), jnp.float32),
    )(parts)


def place_kernel(slot_of, rows_ref, out_ref):
    tile = rows_ref.shape[1]
    for pair in range(out_ref.shape[0] // (2 * tile)):
        both = [rows_ref[slot_of[2 * pair + n]].astype(jnp.float32) for n in range(2)]
        out_ref[2 * tile * pair : 2 * tile * (pair + 1), :] = jnp.concatenate(both).astype(
            out_ref.dtype
        )


def place(slot_of, rows):
    slots, tile, cols = rows.shape
    tiles = slot_of.shape[0]
    return pl.pallas_call(
        place_kernel,
        grid_spec=pltpu.PrefetchScalarGridSpec(
            num_scalar_prefetch=1,
            grid=(1,),
            in_specs=[pl.BlockSpec((slots, tile, cols), lambda i, s: (0, 0, 0))],
            out_specs=pl.BlockSpec((tiles * tile, cols), lambda i, s: (0, 0)),
        ),
        out_shape=jax.ShapeDtypeStruct((tiles * tile, cols), rows.dtype),
        compiler_params=pltpu.CompilerParams(vmem_limit_bytes=32 * 2**20),
    )(slot_of, rows)


def spread(rows, axis):
    copies = jnp.broadcast_to(rows[None], (lax.axis_size(axis),) + rows.shape)
    return lax.all_to_all(copies, axis, 0, 0)


def body(sampled, assignment, inverse_rows, gradient):
    n_zh, n_x, n_yh, n_yl = (lax.axis_size(name) for name in DP)
    held, tile, order = inverse_rows.shape
    tiles = assignment.shape[0]
    tokens, cols = sampled.shape
    width = gradient.shape[1]
    owners = n_zh * n_x * n_yh * n_yl

    ring = n_zh * lax.axis_size("zl")
    hops = [(2 * r, 2 * ((r + 1) % ring)) for r in range(ring)]
    hops += [(2 * r + 1, 2 * ((r - 1) % ring) + 1) for r in range(ring)]
    swap = [(0, 1), (1, 0)]

    def hop(block):
        return lax.ppermute(block, ("zh", "zl", "c"), hops)

    own = sampled.T
    twin = lax.ppermute(own, "c", swap)
    same, cross = [own], [twin]
    for step in range(ring // 2):
        same.append(hop(same[-1]))
        if step < ring // 2 - 1:
            cross.append(hop(cross[-1]))
    far_twin = lax.ppermute(same[-1], "c", swap)

    mine = jnp.dot(
        inverse_rows.reshape(held * tile, order), gradient, preferred_element_type=jnp.float32
    ).astype(jnp.bfloat16)
    other = lax.ppermute(mine, "zh", [(0, 1), (1, 0)])
    first = lax.axis_index("zh") == 0
    rows = jnp.stack([jnp.where(first, mine, other), jnp.where(first, other, mine)])
    rows = spread(rows.reshape(n_zh * held * tile, width), ("yh", "yl"))
    rows = rows.reshape(n_yh * n_yl * n_zh * held * tile, width)
    rows = spread(rows, "x").reshape(owners * held, tile, width)
    far_twin, rows = lax.optimization_barrier((far_twin, rows))
    place_of = jnp.arange(owners * held, dtype=jnp.int32).reshape(n_x, n_yh * n_yl, n_zh, held)
    slot_place = place_of.transpose(2, 0, 1, 3).reshape(-1)
    preconditioned = place(slot_place[assignment], rows)

    near, far = n_x * n_yl, n_yh * n_zh
    index = jnp.arange(tiles, dtype=jnp.int32)
    table = jnp.full((owners * held,), -1, jnp.int32).at[assignment].set(index)
    table = table.reshape(n_zh, n_x, n_yh, n_yl, held).transpose(1, 3, 2, 0, 4).reshape(-1)
    core, upper = lax.axis_index("c"), lax.axis_index("zh")
    here = upper * (ring // n_zh) + lax.axis_index("zl")
    share = cols // n_zh
    more = [upper * share]
    for steps, side in [(n, core) for n in range(ring // 2 + 1)] + [
        (n, 1 - core) for n in range(1, ring // 2)
    ]:
        chip = (here + jnp.where(core == 0, ring - steps, steps)) % ring
        row = (chip % (ring // n_zh) * 2 + side) * cols
        more += [row, (chip // (ring // n_zh) != upper).astype(jnp.int32)]
    table = jnp.concatenate([table, jnp.stack(more).astype(jnp.int32)])
    keep, send = gram(
        table, own, twin, far_twin, same[1:] + cross[1:], near, far * held, tile, share
    )
    terms = keep + lax.ppermute(send, "c", swap)
    terms = jnp.sum(lax.all_to_all(terms, NEAR, 0, 0), axis=0)
    terms = lax.all_to_all(terms.reshape(far, -1, terms.shape[1]), FAR, 0, 0)
    terms = terms.reshape((n_yh, n_zh) + terms.shape[1:])
    factor_tiles = sum_join(terms, held, tile, cols, 1.0 / (tokens * owners))
    return factor_tiles, preconditioned


def solution(mesh):
    split = Mesh(mesh.devices.reshape(2, 4, 4, 2, 4, 2), DP + GROUP)
    placed = (P(DP, GROUP), P(), P(DP, None, None), P(None, GROUP))
    return jax.shard_map(
        body,
        mesh=split,
        in_specs=placed,
        out_specs=(P(DP, None, GROUP), P(None, GROUP)),
        check_vma=False,
    )
```

```python
import functools

import jax
import jax.numpy as jnp
from jax import lax
from jax.experimental import pallas as pl
from jax.experimental.pallas import tpu as pltpu
from jax.sharding import Mesh, PartitionSpec as P

DP = ("zh", "x", "yh", "yl")
GROUP = ("zl", "c")
Y = ("yh", "yl")


def gram_kernel(table, slots, near_ref, far_ref, *refs):
    *blocks, out_ref, total = refs
    cols = near_ref.shape[0]
    share = total.shape[1]
    dest = pl.program_id(0)
    pairs = slots // 2
    high = out_ref.shape[1] // pairs
    tile = (high - 8) // 2
    count = pl.num_programs(0) * slots

    @pl.when(dest == 0)
    def _():
        mine = pl.ds(pl.multiple_of(table[count], 16), share)
        total[...] = jnp.zeros_like(total)
        for n, block in enumerate(blocks):
            at = pl.ds(pl.multiple_of(table[count + 1 + 2 * n], 8), cols)
            near = table[count + 2 + 2 * n] == 0
            factor = jnp.where(near, near_ref[mine, :], far_ref[mine, :])
            total[at, :] += lax.dot_general(
                block[...], factor, (((1,), (1,)), ((), ())), preferred_element_type=jnp.float32
            )

    for pair in range(pairs):
        both = []
        for n in range(2):
            t = table[dest * slots + 2 * pair + n]
            rows = total[pl.ds(pl.multiple_of(jnp.maximum(t, 0) * tile, 8), tile), :]
            both.append(jnp.where(t >= 0, rows, 0.0))
        out_ref[0, high * pair : high * (pair + 1), :] = pack(jnp.concatenate(both))


def pack(rows):
    n, cols = rows.shape
    rest = [rows[8 * k : 8 * k + 8, 128:] for k in range(n // 8)]
    rest.append(jnp.zeros((8, 128 - (cols - 128) * (n // 8)), rows.dtype))
    return jnp.concatenate([rows[:, :128], jnp.concatenate(rest, axis=1)])


def gram(table, near, far, blocks, dests, slots, tile, share):
    cols, tokens = near.shape
    high = 2 * tile + 8
    out = jax.ShapeDtypeStruct((dests, slots // 2 * high, 128), jnp.float32)
    given = [near, far, *blocks]
    return pl.pallas_call(
        lambda table_ref, *refs: gram_kernel(table_ref, slots, *refs),
        grid_spec=pltpu.PrefetchScalarGridSpec(
            num_scalar_prefetch=1,
            grid=(dests,),
            in_specs=[pl.BlockSpec((cols, tokens), lambda d, t: (0, 0))] * len(given),
            out_specs=pl.BlockSpec((1,) + out.shape[1:], lambda d, t: (d, 0, 0)),
            scratch_shapes=[pltpu.VMEM((len(blocks) * cols, share), jnp.float32)],
        ),
        out_shape=out,
        compiler_params=pltpu.CompilerParams(vmem_limit_bytes=48 * 2**20),
    )(table, *given)


def sum_join_kernel(scale, parts_ref, out_ref):
    held, tile, cols = out_ref.shape
    halves, rows = parts_ref.shape[0], held * tile
    extra = cols // halves - 128
    pieces = []
    for half in range(halves):
        total = parts_ref[half, 0]
        for n in range(1, parts_ref.shape[1]):
            total = total + parts_ref[half, n]
        total = total * scale
        pieces.append(total[:rows])
        rest = total[rows:]
        pieces.append(
            jnp.concatenate([rest[:, extra * n : extra * (n + 1)] for n in range(rows // 8)])
        )
    joined = jnp.concatenate(pieces, axis=1)
    for slot in range(held):
        out_ref[slot] = joined[tile * slot : tile * (slot + 1)]


def sum_join(parts, held, tile, cols, scale):
    return pl.pallas_call(
        functools.partial(sum_join_kernel, scale),
        out_shape=jax.ShapeDtypeStruct((held, tile, cols), jnp.float32),
    )(parts)


def place_kernel(slot_of, rows_ref, out_ref):
    tile = rows_ref.shape[1]
    for pair in range(out_ref.shape[0] // (2 * tile)):
        both = [rows_ref[slot_of[2 * pair + n]].astype(jnp.float32) for n in range(2)]
        out_ref[2 * tile * pair : 2 * tile * (pair + 1), :] = jnp.concatenate(both).astype(
            out_ref.dtype
        )


def place(slot_of, rows):
    slots, tile, cols = rows.shape
    tiles = slot_of.shape[0]
    return pl.pallas_call(
        place_kernel,
        grid_spec=pltpu.PrefetchScalarGridSpec(
            num_scalar_prefetch=1,
            grid=(1,),
            in_specs=[pl.BlockSpec((slots, tile, cols), lambda i, s: (0, 0, 0))],
            out_specs=pl.BlockSpec((tiles * tile, cols), lambda i, s: (0, 0)),
        ),
        out_shape=jax.ShapeDtypeStruct((tiles * tile, cols), rows.dtype),
        compiler_params=pltpu.CompilerParams(vmem_limit_bytes=32 * 2**20),
    )(slot_of, rows)


def spread(rows, axis):
    copies = jnp.broadcast_to(rows[None], (lax.axis_size(axis),) + rows.shape)
    return lax.all_to_all(copies, axis, 0, 0)


def body(sampled, assignment, inverse_rows, gradient):
    n_zh, n_x, n_yh, n_yl = (lax.axis_size(name) for name in DP)
    held, tile, order = inverse_rows.shape
    tiles = assignment.shape[0]
    tokens, cols = sampled.shape
    width = gradient.shape[1]
    owners = n_zh * n_x * n_yh * n_yl

    ring = n_zh * lax.axis_size("zl")
    hops = [(2 * r, 2 * ((r + 1) % ring)) for r in range(ring)]
    hops += [(2 * r + 1, 2 * ((r - 1) % ring) + 1) for r in range(ring)]
    swap = [(0, 1), (1, 0)]

    def hop(block):
        return lax.ppermute(block, ("zh", "zl", "c"), hops)

    own = sampled.T
    twin = lax.ppermute(own, "c", swap)
    same, cross = [own], [twin]
    for step in range(ring // 2):
        same.append(hop(same[-1]))
        if step < ring // 2 - 1:
            cross.append(hop(cross[-1]))
    far_twin = lax.ppermute(same[-1], "c", swap)

    mine = jnp.dot(
        inverse_rows.reshape(held * tile, order), gradient, preferred_element_type=jnp.float32
    ).astype(jnp.bfloat16)
    other = lax.ppermute(mine, "zh", [(0, 1), (1, 0)])
    first = lax.axis_index("zh") == 0
    rows = jnp.stack([jnp.where(first, mine, other), jnp.where(first, other, mine)])
    rows = spread(rows.reshape(n_zh * held * tile, width), Y)
    rows = rows.reshape(n_yh * n_yl * n_zh * held * tile, width)
    rows, cross[2] = lax.optimization_barrier((rows, cross[2]))
    rows = spread(rows, "x").reshape(owners * held, tile, width)
    far_twin, rows = lax.optimization_barrier((far_twin, rows))
    place_of = jnp.arange(owners * held, dtype=jnp.int32).reshape(n_x, n_yh * n_yl, n_zh, held)
    slot_place = place_of.transpose(2, 0, 1, 3).reshape(-1)
    preconditioned = place(slot_place[assignment], rows)

    n_y = n_yh * n_yl
    index = jnp.arange(tiles, dtype=jnp.int32)
    table = jnp.full((owners * held,), -1, jnp.int32).at[assignment].set(index)
    table = table.reshape(n_zh, n_x, n_y, held).transpose(1, 0, 2, 3).reshape(-1)
    core, upper = lax.axis_index("c"), lax.axis_index("zh")
    here = upper * (ring // n_zh) + lax.axis_index("zl")
    share = cols // n_zh
    more = [upper * share]
    for steps, side in [(n, core) for n in range(ring // 2 + 1)] + [
        (n, 1 - core) for n in range(1, ring // 2)
    ]:
        chip = (here + jnp.where(core == 0, ring - steps, steps)) % ring
        row = (chip % (ring // n_zh) * 2 + side) * cols
        more += [row, (chip // (ring // n_zh) != upper).astype(jnp.int32)]
    table = jnp.concatenate([table, jnp.stack(more).astype(jnp.int32)])
    blocks = same + cross[1:]
    sizes = (n_x, n_zh * n_y * held, tile, share)
    send = gram(table, twin, far_twin, blocks, *sizes)
    received = lax.ppermute(send, "c", swap)
    terms = gram(table, own, same[-1], blocks, *sizes) + received
    terms = jnp.sum(lax.all_to_all(terms, "x", 0, 0), axis=0)
    terms = lax.all_to_all(terms.reshape(n_zh * n_y, -1, terms.shape[1]), ("zh",) + Y, 0, 0)
    terms = terms.reshape((n_zh, n_y) + terms.shape[1:])
    factor_tiles = sum_join(terms, held, tile, cols, 1.0 / (tokens * owners))
    return factor_tiles, preconditioned


def solution(mesh):
    split = Mesh(mesh.devices.reshape(2, 4, 4, 2, 4, 2), DP + GROUP)
    placed = (P(DP, GROUP), P(), P(DP, None, None), P(None, GROUP))
    return jax.shard_map(
        body,
        mesh=split,
        in_specs=placed,
        out_specs=(P(DP, None, GROUP), P(None, GROUP)),
        check_vma=False,
    )
```

```python
import functools

import jax
import jax.numpy as jnp
from jax import lax
from jax.experimental import pallas as pl
from jax.experimental.pallas import tpu as pltpu
from jax.sharding import Mesh, PartitionSpec as P

DP = ("zh", "x", "yh", "yl")
GROUP = ("zl", "c")
Y = ("yh", "yl")
NEAR = ("x", "yl")
FAR = ("yh", "zh")


def gram_kernel(table, slots, near_ref, far_ref, *refs):
    *blocks, out_ref, total = refs
    cols = near_ref.shape[0]
    share = total.shape[1]
    dest = pl.program_id(0)
    pairs = slots // 2
    high = out_ref.shape[1] // pairs
    tile = (high - 8) // 2
    count = pl.num_programs(0) * slots

    @pl.when(dest == 0)
    def _():
        mine = pl.ds(pl.multiple_of(table[count], 16), share)
        total[...] = jnp.zeros_like(total)
        for n, block in enumerate(blocks):
            at = pl.ds(pl.multiple_of(table[count + 1 + 2 * n], 8), cols)
            near = table[count + 2 + 2 * n] == 0
            factor = jnp.where(near, near_ref[mine, :], far_ref[mine, :])
            total[at, :] += lax.dot_general(
                block[...], factor, (((1,), (1,)), ((), ())), preferred_element_type=jnp.float32
            )

    for pair in range(pairs):
        both = []
        for n in range(2):
            t = table[dest * slots + 2 * pair + n]
            rows = total[pl.ds(pl.multiple_of(jnp.maximum(t, 0) * tile, 8), tile), :]
            both.append(jnp.where(t >= 0, rows, 0.0))
        out_ref[0, high * pair : high * (pair + 1), :] = pack(jnp.concatenate(both))


def pack(rows):
    n, cols = rows.shape
    rest = [rows[8 * k : 8 * k + 8, 128:] for k in range(n // 8)]
    rest.append(jnp.zeros((8, 128 - (cols - 128) * (n // 8)), rows.dtype))
    return jnp.concatenate([rows[:, :128], jnp.concatenate(rest, axis=1)])


def gram(table, near, far, blocks, dests, slots, tile, share):
    cols, tokens = near.shape
    high = 2 * tile + 8
    out = jax.ShapeDtypeStruct((dests, slots // 2 * high, 128), jnp.float32)
    given = [near, far, *blocks]
    return pl.pallas_call(
        lambda table_ref, *refs: gram_kernel(table_ref, slots, *refs),
        grid_spec=pltpu.PrefetchScalarGridSpec(
            num_scalar_prefetch=1,
            grid=(dests,),
            in_specs=[pl.BlockSpec((cols, tokens), lambda d, t: (0, 0))] * len(given),
            out_specs=pl.BlockSpec((1,) + out.shape[1:], lambda d, t: (d, 0, 0)),
            scratch_shapes=[pltpu.VMEM((len(blocks) * cols, share), jnp.float32)],
        ),
        out_shape=out,
        compiler_params=pltpu.CompilerParams(vmem_limit_bytes=24 * 2**20),
    )(table, *given)


def sum_join_kernel(scale, parts_ref, out_ref):
    held, tile, cols = out_ref.shape
    halves, rows = parts_ref.shape[1], held * tile
    extra = cols // halves - 128
    pieces = []
    for half in range(halves):
        total = parts_ref[0, half]
        for n in range(1, parts_ref.shape[0]):
            total = total + parts_ref[n, half]
        total = total * scale
        pieces.append(total[:rows])
        rest = total[rows:]
        pieces.append(
            jnp.concatenate([rest[:, extra * n : extra * (n + 1)] for n in range(rows // 8)])
        )
    joined = jnp.concatenate(pieces, axis=1)
    for slot in range(held):
        out_ref[slot] = joined[tile * slot : tile * (slot + 1)]


def sum_join(parts, held, tile, cols, scale):
    return pl.pallas_call(
        functools.partial(sum_join_kernel, scale),
        out_shape=jax.ShapeDtypeStruct((held, tile, cols), jnp.float32),
    )(parts)


def place_kernel(place_of, rows_ref, late_ref, out_ref):
    tile = rows_ref.shape[1]
    cols = out_ref.shape[1]
    tiles = out_ref.shape[0] // tile
    for pair in range(tiles // 2):
        both = []
        for n in range(2):
            at, theirs = place_of[2 * pair + n], place_of[tiles + 2 * pair + n]
            rows = rows_ref[at].astype(jnp.float32)
            other = jnp.concatenate(
                [rows[:, cols:], late_ref[at].astype(jnp.float32)], axis=1
            )
            both.append(jnp.where(theirs > 0, other, rows[:, :cols]))
        out_ref[2 * tile * pair : 2 * tile * (pair + 1), :] = jnp.concatenate(both).astype(
            out_ref.dtype
        )


def place(place_of, rows, late):
    tile = rows.shape[1]
    cols = (rows.shape[2] + late.shape[2]) // 2
    tiles = place_of.shape[0] // 2
    return pl.pallas_call(
        place_kernel,
        grid_spec=pltpu.PrefetchScalarGridSpec(
            num_scalar_prefetch=1,
            grid=(1,),
            in_specs=[
                pl.BlockSpec(rows.shape, lambda i, s: (0, 0, 0)),
                pl.BlockSpec(late.shape, lambda i, s: (0, 0, 0)),
            ],
            out_specs=pl.BlockSpec((tiles * tile, cols), lambda i, s: (0, 0)),
        ),
        out_shape=jax.ShapeDtypeStruct((tiles * tile, cols), rows.dtype),
        compiler_params=pltpu.CompilerParams(vmem_limit_bytes=24 * 2**20),
    )(place_of, rows, late)


def spread(rows, axis):
    copies = jnp.broadcast_to(rows[None], (lax.axis_size(axis),) + rows.shape)
    return lax.all_to_all(copies, axis, 0, 0)


def body(sampled, assignment, inverse_rows, gradient):
    n_zh, n_x, n_yh, n_yl = (lax.axis_size(name) for name in DP)
    held, tile, order = inverse_rows.shape
    tiles = assignment.shape[0]
    tokens, cols = sampled.shape
    width = gradient.shape[1]
    owners = n_zh * n_x * n_yh * n_yl

    ring = n_zh * lax.axis_size("zl")
    hops = [(2 * r, 2 * ((r + 1) % ring)) for r in range(ring)]
    hops += [(2 * r + 1, 2 * ((r - 1) % ring) + 1) for r in range(ring)]
    swap = [(0, 1), (1, 0)]

    def hop(block):
        return lax.ppermute(block, ("zh", "zl", "c"), hops)

    owner_slots = owners * held
    index = jnp.arange(tiles, dtype=jnp.int32)
    table = jnp.full((owner_slots,), -1, jnp.int32).at[assignment].set(index)
    table = table.reshape(n_zh, n_x, n_yh, n_yl, held).transpose(1, 3, 2, 0, 4).reshape(-1)
    core, upper = lax.axis_index("c"), lax.axis_index("zh")
    here = upper * (ring // n_zh) + lax.axis_index("zl")
    share = cols // n_zh
    more = [upper * share]
    for steps, side in [(n, core) for n in range(ring // 2 + 1)] + [
        (n, 1 - core) for n in range(1, ring // 2)
    ]:
        chip = (here + jnp.where(core == 0, ring - steps, steps)) % ring
        row = (chip % (ring // n_zh) * 2 + side) * cols
        more += [row, (chip // (ring // n_zh) != upper).astype(jnp.int32)]
    table = jnp.concatenate([table, jnp.stack(more).astype(jnp.int32)])

    own = sampled.T
    twin = lax.ppermute(own, "c", swap)
    same, cross = [own, hop(own)], [twin, hop(twin)]

    inverse_rows, twin = lax.optimization_barrier((inverse_rows, twin))
    rows = jnp.dot(
        inverse_rows.reshape(held * tile, order), gradient, preferred_element_type=jnp.float32
    ).astype(jnp.bfloat16)
    early = width * 2 // 3 // 128 * 128
    other = lax.ppermute(rows[:, :early], "zh", swap)
    same[1], other, table = lax.optimization_barrier((same[1], other, table))
    for step in range(1, ring // 2 - 1):
        same.append(hop(same[-1]))
        cross.append(hop(cross[-1]))
    rows = spread(jnp.concatenate([rows, other], axis=1), Y)
    rows = spread(rows.reshape(-1, width + early), "x")
    same.append(hop(same[-1]))
    same[-1], cross[-1] = lax.optimization_barrier((same[-1], cross[-1]))
    far_twin = lax.ppermute(same[-1], "c", swap)
    far_twin, rows = lax.optimization_barrier((far_twin, rows))
    rows = rows.reshape(-1, tile, width + early)
    late = lax.ppermute(rows[:, :, early:width], "zh", swap)

    blocks = same + cross[1:]
    near, far = n_x * n_yl, n_yh * n_zh
    sizes = (near, far * held, tile, share)
    send = gram(table, twin, far_twin, blocks, *sizes)
    received = lax.ppermute(send, "c", swap)
    terms = gram(table, own, same[-1], blocks, *sizes) + received
    terms = lax.all_to_all(terms, NEAR, 0, 0)
    terms = functools.reduce(jnp.add, [terms[n] for n in range(near)])
    terms, late = lax.optimization_barrier((terms, late))
    terms = lax.all_to_all(terms.reshape(far, -1, terms.shape[1]), FAR, 0, 0)
    terms = terms.reshape((n_yh, n_zh) + terms.shape[1:])
    factor_tiles = sum_join(terms, held, tile, cols, 1.0 / (tokens * owners))

    half = owner_slots // n_zh
    theirs = (assignment // half != upper).astype(jnp.int32)
    place_of = jnp.concatenate([assignment % half, theirs]).astype(jnp.int32)
    preconditioned = place(place_of, rows, late)
    return factor_tiles, preconditioned


def solution(mesh):
    split = Mesh(mesh.devices.reshape(2, 4, 4, 2, 4, 2), DP + GROUP)
    placed = (P(DP, GROUP), P(), P(DP, None, None), P(None, GROUP))
    return jax.shard_map(
        body,
        mesh=split,
        in_specs=placed,
        out_specs=(P(DP, None, GROUP), P(None, GROUP)),
        check_vma=False,
    )
```

```python
import functools

import jax
import jax.numpy as jnp
from jax import lax
from jax.experimental import pallas as pl
from jax.experimental.pallas import tpu as pltpu
from jax.sharding import Mesh, PartitionSpec as P

DP = ("zh", "x", "yh", "yl")
GROUP = ("zl", "c")
Y = ("yh", "yl")


def gram_kernel(table, slots, near_ref, far_ref, *refs):
    *blocks, out_ref, total = refs
    cols = near_ref.shape[0]
    share = total.shape[1]
    dest = pl.program_id(0)
    pairs = slots // 2
    high = out_ref.shape[1] // pairs
    tile = (high - 8) // 2
    count = pl.num_programs(0) * slots

    @pl.when(dest == 0)
    def _():
        mine = pl.ds(pl.multiple_of(table[count], 16), share)
        total[...] = jnp.zeros_like(total)
        for n, block in enumerate(blocks):
            at = pl.ds(pl.multiple_of(table[count + 1 + 2 * n], 8), cols)
            near = table[count + 2 + 2 * n] == 0
            factor = jnp.where(near, near_ref[mine, :], far_ref[mine, :])
            total[at, :] += lax.dot_general(
                block[...], factor, (((1,), (1,)), ((), ())), preferred_element_type=jnp.float32
            )

    for pair in range(pairs):
        both = []
        for n in range(2):
            t = table[dest * slots + 2 * pair + n]
            rows = total[pl.ds(pl.multiple_of(jnp.maximum(t, 0) * tile, 8), tile), :]
            both.append(jnp.where(t >= 0, rows, 0.0))
        out_ref[0, high * pair : high * (pair + 1), :] = pack(jnp.concatenate(both))


def pack(rows):
    n, cols = rows.shape
    rest = [rows[8 * k : 8 * k + 8, 128:] for k in range(n // 8)]
    rest.append(jnp.zeros((8, 128 - (cols - 128) * (n // 8)), rows.dtype))
    return jnp.concatenate([rows[:, :128], jnp.concatenate(rest, axis=1)])


def gram(table, near, far, blocks, dests, slots, tile, share):
    cols, tokens = near.shape
    high = 2 * tile + 8
    out = jax.ShapeDtypeStruct((dests, slots // 2 * high, 128), jnp.float32)
    given = [near, far, *blocks]
    return pl.pallas_call(
        lambda table_ref, *refs: gram_kernel(table_ref, slots, *refs),
        grid_spec=pltpu.PrefetchScalarGridSpec(
            num_scalar_prefetch=1,
            grid=(dests,),
            in_specs=[pl.BlockSpec((cols, tokens), lambda d, t: (0, 0))] * len(given),
            out_specs=pl.BlockSpec((1,) + out.shape[1:], lambda d, t: (d, 0, 0)),
            scratch_shapes=[pltpu.VMEM((len(blocks) * cols, share), jnp.float32)],
        ),
        out_shape=out,
        compiler_params=pltpu.CompilerParams(vmem_limit_bytes=24 * 2**20),
    )(table, *given)


def sum_join_kernel(scale, parts_ref, out_ref):
    held, tile, cols = out_ref.shape
    halves, rows = parts_ref.shape[0], held * tile
    extra = cols // halves - 128
    pieces = []
    for half in range(halves):
        total = parts_ref[half, 0]
        for n in range(1, parts_ref.shape[1]):
            total = total + parts_ref[half, n]
        total = total * scale
        pieces.append(total[:rows])
        rest = total[rows:]
        pieces.append(
            jnp.concatenate([rest[:, extra * n : extra * (n + 1)] for n in range(rows // 8)])
        )
    joined = jnp.concatenate(pieces, axis=1)
    for slot in range(held):
        out_ref[slot] = joined[tile * slot : tile * (slot + 1)]


def sum_join(parts, held, tile, cols, scale):
    return pl.pallas_call(
        functools.partial(sum_join_kernel, scale),
        out_shape=jax.ShapeDtypeStruct((held, tile, cols), jnp.float32),
    )(parts)


def place_kernel(place_of, *refs):
    *blocks, out_ref, rows_ref = refs
    tile = rows_ref.shape[1]
    at = 0
    for block in blocks:
        rows_ref[at : at + block.shape[0]] = block[...]
        at += block.shape[0]
    for pair in range(out_ref.shape[0] // (2 * tile)):
        both = [rows_ref[place_of[2 * pair + n]].astype(jnp.float32) for n in range(2)]
        out_ref[2 * tile * pair : 2 * tile * (pair + 1), :] = jnp.concatenate(both).astype(
            out_ref.dtype
        )


def place(place_of, blocks):
    _, tile, cols = blocks[0].shape
    slots = sum(block.shape[0] for block in blocks)
    tiles = place_of.shape[0]
    return pl.pallas_call(
        place_kernel,
        grid_spec=pltpu.PrefetchScalarGridSpec(
            num_scalar_prefetch=1,
            grid=(1,),
            in_specs=[pl.BlockSpec(block.shape, lambda i, s: (0, 0, 0)) for block in blocks],
            out_specs=pl.BlockSpec((tiles * tile, cols), lambda i, s: (0, 0)),
            scratch_shapes=[pltpu.VMEM((slots, tile, cols), blocks[0].dtype)],
        ),
        out_shape=jax.ShapeDtypeStruct((tiles * tile, cols), blocks[0].dtype),
        compiler_params=pltpu.CompilerParams(vmem_limit_bytes=20 * 2**20),
    )(place_of, *blocks)


def spread(rows, axis):
    copies = jnp.broadcast_to(rows[None], (lax.axis_size(axis),) + rows.shape)
    return lax.all_to_all(copies, axis, 0, 0)


def body(sampled, assignment, inverse_rows, gradient):
    n_zh, n_x, n_yh, n_yl = (lax.axis_size(name) for name in DP)
    held, tile, order = inverse_rows.shape
    tiles = assignment.shape[0]
    tokens, cols = sampled.shape
    width = gradient.shape[1]
    owners = n_zh * n_x * n_yh * n_yl

    ring = n_zh * lax.axis_size("zl")
    hops = [(2 * r, 2 * ((r + 1) % ring)) for r in range(ring)]
    hops += [(2 * r + 1, 2 * ((r - 1) % ring) + 1) for r in range(ring)]
    swap = [(0, 1), (1, 0)]

    def hop(block):
        return lax.ppermute(block, ("zh", "zl", "c"), hops)

    owner_slots = owners * held
    index = jnp.arange(tiles, dtype=jnp.int32)
    table = jnp.full((owner_slots,), -1, jnp.int32).at[assignment].set(index)
    table = table.reshape(n_zh, n_x, n_yh, n_yl, held).transpose(1, 0, 2, 3, 4).reshape(-1)
    core, upper = lax.axis_index("c"), lax.axis_index("zh")
    here = upper * (ring // n_zh) + lax.axis_index("zl")
    share = cols // n_zh
    more = [upper * share]
    for steps, side in [(n, core) for n in range(ring // 2 + 1)] + [
        (n, 1 - core) for n in range(1, ring // 2)
    ]:
        chip = (here + jnp.where(core == 0, ring - steps, steps)) % ring
        row = (chip % (ring // n_zh) * 2 + side) * cols
        more += [row, (chip // (ring // n_zh) != upper).astype(jnp.int32)]
    table = jnp.concatenate([table, jnp.stack(more).astype(jnp.int32)])

    own = sampled.T
    twin = lax.ppermute(own, "c", swap)
    same, cross = [own, hop(own)], [twin, hop(twin)]

    inverse_rows, twin = lax.optimization_barrier((inverse_rows, twin))
    mine = jnp.dot(
        inverse_rows.reshape(held * tile, order), gradient, preferred_element_type=jnp.float32
    ).astype(jnp.bfloat16)
    other = lax.ppermute(mine, "zh", swap)
    same[1], other, table = lax.optimization_barrier((same[1], other, table))
    rows = jnp.where(upper == 0, jnp.stack([mine, other]), jnp.stack([other, mine]))
    rows = spread(rows.reshape(n_zh * held * tile, width), "x")
    same.append(hop(same[1]))
    cross.append(hop(cross[1]))
    same[2], rows = lax.optimization_barrier((same[2], rows))
    rows = rows.reshape(-1, tile, width)
    n_y = n_yh * n_yl
    up = [(n, (n + 1) % n_y) for n in range(n_y)]
    down = [(n, (n - 1) % n_y) for n in range(n_y)]
    below, above = [rows], [rows]

    def pass_on():
        below.append(lax.ppermute(below[-1], Y, up))
        if len(below) <= n_y // 2:
            above.append(lax.ppermute(above[-1], Y, down))

    pass_on()
    for step in range(2, ring // 2):
        if step == ring // 2 - 1:
            same[-1], below[1], above[1] = lax.optimization_barrier((same[-1], below[1], above[1]))
        same.append(hop(same[-1]))
        if step < ring // 2 - 1:
            cross.append(hop(cross[-1]))
    same[-1], cross[-1] = lax.optimization_barrier((same[-1], cross[-1]))
    pass_on()
    same[-1], below[2], above[2] = lax.optimization_barrier((same[-1], below[2], above[2]))
    far_twin = lax.ppermute(same[-1], "c", swap)
    pass_on()
    pass_on()

    blocks = same + cross[1:]
    near, far = n_x, n_zh * n_y
    sizes = (near, far * held, tile, share)
    send = gram(table, twin, far_twin, blocks, *sizes)
    received = lax.ppermute(send, "c", swap)
    terms = gram(table, own, same[-1], blocks, *sizes) + received
    terms = lax.all_to_all(terms, "x", 0, 0)
    terms = functools.reduce(jnp.add, [terms[n] for n in range(near)])
    terms, below[-1], above[-1] = lax.optimization_barrier((terms, below[-1], above[-1]))
    terms = lax.all_to_all(terms.reshape(far, -1, terms.shape[1]), ("zh",) + Y, 0, 0)
    terms = terms.reshape((n_zh, n_y) + terms.shape[1:])
    factor_tiles = sum_join(terms, held, tile, cols, 1.0 / (tokens * owners))

    owner, slot = assignment // held, assignment % held
    down_by = (lax.axis_index(Y) - owner) % n_y
    place_of = (down_by * n_x + owner // n_y % n_x) * n_zh + owner // (n_y * n_x)
    preconditioned = place(
        (place_of * held + slot).astype(jnp.int32), below + above[:0:-1]
    )
    return factor_tiles, preconditioned


def solution(mesh):
    split = Mesh(mesh.devices.reshape(2, 4, 4, 2, 4, 2), DP + GROUP)
    placed = (P(DP, GROUP), P(), P(DP, None, None), P(None, GROUP))
    return jax.shard_map(
        body,
        mesh=split,
        in_specs=placed,
        out_specs=(P(DP, None, GROUP), P(None, GROUP)),
        check_vma=False,
    )
```

```python
import functools

import jax
import jax.numpy as jnp
from jax import lax
from jax.experimental import pallas as pl
from jax.experimental.pallas import tpu as pltpu
from jax.sharding import Mesh, PartitionSpec as P

DP = ("zh", "x", "yh", "yl")
GROUP = ("zl", "c")
Y = ("yh", "yl")


def gram_kernel(table, slots, near_ref, far_ref, *refs):
    *blocks, out_ref, total = refs
    cols = near_ref.shape[0]
    share = total.shape[1]
    dest = pl.program_id(0)
    pairs = slots // 2
    high = out_ref.shape[1] // pairs
    tile = (high - 8) // 2
    count = pl.num_programs(0) * slots

    @pl.when(dest == 0)
    def _():
        mine = pl.ds(pl.multiple_of(table[count], 16), share)
        total[...] = jnp.zeros_like(total)
        for n, block in enumerate(blocks):
            at = pl.ds(pl.multiple_of(table[count + 1 + 2 * n], 8), cols)
            near = table[count + 2 + 2 * n] == 0
            factor = jnp.where(near, near_ref[mine, :], far_ref[mine, :])
            total[at, :] += lax.dot_general(
                block[...], factor, (((1,), (1,)), ((), ())), preferred_element_type=jnp.float32
            )

    for pair in range(pairs):
        both = []
        for n in range(2):
            t = table[dest * slots + 2 * pair + n]
            rows = total[pl.ds(pl.multiple_of(jnp.maximum(t, 0) * tile, 8), tile), :]
            both.append(jnp.where(t >= 0, rows, 0.0))
        out_ref[0, high * pair : high * (pair + 1), :] = pack(jnp.concatenate(both))


def pack(rows):
    n, cols = rows.shape
    rest = [rows[8 * k : 8 * k + 8, 128:] for k in range(n // 8)]
    rest.append(jnp.zeros((8, 128 - (cols - 128) * (n // 8)), rows.dtype))
    return jnp.concatenate([rows[:, :128], jnp.concatenate(rest, axis=1)])


def gram(table, near, far, blocks, dests, slots, tile, share):
    cols, tokens = near.shape
    high = 2 * tile + 8
    out = jax.ShapeDtypeStruct((dests, slots // 2 * high, 128), jnp.float32)
    given = [near, far, *blocks]
    return pl.pallas_call(
        lambda table_ref, *refs: gram_kernel(table_ref, slots, *refs),
        grid_spec=pltpu.PrefetchScalarGridSpec(
            num_scalar_prefetch=1,
            grid=(dests,),
            in_specs=[pl.BlockSpec((cols, tokens), lambda d, t: (0, 0))] * len(given),
            out_specs=pl.BlockSpec((1,) + out.shape[1:], lambda d, t: (d, 0, 0)),
            scratch_shapes=[pltpu.VMEM((len(blocks) * cols, share), jnp.float32)],
        ),
        out_shape=out,
        compiler_params=pltpu.CompilerParams(vmem_limit_bytes=24 * 2**20),
    )(table, *given)


def sum_join_kernel(scale, parts_ref, out_ref):
    held, tile, cols = out_ref.shape
    halves, rows = parts_ref.shape[0], held * tile
    extra = cols // halves - 128
    pieces = []
    for half in range(halves):
        total = parts_ref[half, 0]
        for n in range(1, parts_ref.shape[1]):
            total = total + parts_ref[half, n]
        total = total * scale
        pieces.append(total[:rows])
        rest = total[rows:]
        pieces.append(
            jnp.concatenate([rest[:, extra * n : extra * (n + 1)] for n in range(rows // 8)])
        )
    joined = jnp.concatenate(pieces, axis=1)
    for slot in range(held):
        out_ref[slot] = joined[tile * slot : tile * (slot + 1)]


def sum_join(parts, held, tile, cols, scale):
    return pl.pallas_call(
        functools.partial(sum_join_kernel, scale),
        out_shape=jax.ShapeDtypeStruct((held, tile, cols), jnp.float32),
    )(parts)


def place_kernel(place_of, *refs):
    *blocks, out_ref, rows_ref = refs
    tile = rows_ref.shape[1]
    at = 0
    for block in blocks:
        rows_ref[at : at + block.shape[0]] = block[...]
        at += block.shape[0]
    for pair in range(out_ref.shape[0] // (2 * tile)):
        both = [rows_ref[place_of[2 * pair + n]].astype(jnp.float32) for n in range(2)]
        out_ref[2 * tile * pair : 2 * tile * (pair + 1), :] = jnp.concatenate(both).astype(
            out_ref.dtype
        )


def place(place_of, blocks):
    _, tile, cols = blocks[0].shape
    slots = sum(block.shape[0] for block in blocks)
    tiles = place_of.shape[0]
    return pl.pallas_call(
        place_kernel,
        grid_spec=pltpu.PrefetchScalarGridSpec(
            num_scalar_prefetch=1,
            grid=(1,),
            in_specs=[pl.BlockSpec(block.shape, lambda i, s: (0, 0, 0)) for block in blocks],
            out_specs=pl.BlockSpec((tiles * tile, cols), lambda i, s: (0, 0)),
            scratch_shapes=[pltpu.VMEM((slots, tile, cols), blocks[0].dtype)],
        ),
        out_shape=jax.ShapeDtypeStruct((tiles * tile, cols), blocks[0].dtype),
        compiler_params=pltpu.CompilerParams(vmem_limit_bytes=20 * 2**20),
    )(place_of, *blocks)


def spread(rows, axis):
    copies = jnp.broadcast_to(rows[None], (lax.axis_size(axis),) + rows.shape)
    return lax.all_to_all(copies, axis, 0, 0)


def body(sampled, assignment, inverse_rows, gradient):
    n_zh, n_x, n_yh, n_yl = (lax.axis_size(name) for name in DP)
    held, tile, order = inverse_rows.shape
    tiles = assignment.shape[0]
    tokens, cols = sampled.shape
    width = gradient.shape[1]
    owners = n_zh * n_x * n_yh * n_yl

    ring = n_zh * lax.axis_size("zl")
    hops = [(2 * r, 2 * ((r + 1) % ring)) for r in range(ring)]
    hops += [(2 * r + 1, 2 * ((r - 1) % ring) + 1) for r in range(ring)]
    swap = [(0, 1), (1, 0)]

    def hop(block):
        return lax.ppermute(block, ("zh", "zl", "c"), hops)

    owner_slots = owners * held
    index = jnp.arange(tiles, dtype=jnp.int32)
    table = jnp.full((owner_slots,), -1, jnp.int32).at[assignment].set(index)
    table = table.reshape(n_zh, n_x, n_yh, n_yl, held).transpose(1, 0, 2, 3, 4).reshape(-1)
    core, upper = lax.axis_index("c"), lax.axis_index("zh")
    here = upper * (ring // n_zh) + lax.axis_index("zl")
    share = cols // n_zh
    more = [upper * share]
    for steps, side in [(n, core) for n in range(ring // 2 + 1)] + [
        (n, 1 - core) for n in range(1, ring // 2)
    ]:
        chip = (here + jnp.where(core == 0, ring - steps, steps)) % ring
        row = (chip % (ring // n_zh) * 2 + side) * cols
        more += [row, (chip // (ring // n_zh) != upper).astype(jnp.int32)]
    table = jnp.concatenate([table, jnp.stack(more).astype(jnp.int32)])

    own = sampled.T
    twin = lax.ppermute(own, "c", swap)
    same, cross = [own, hop(own)], [twin, hop(twin)]

    inverse_rows, twin = lax.optimization_barrier((inverse_rows, twin))
    mine = jnp.dot(
        inverse_rows.reshape(held * tile, order), gradient, preferred_element_type=jnp.float32
    ).astype(jnp.bfloat16)
    other = lax.ppermute(mine, "zh", swap)
    same[1], other, table = lax.optimization_barrier((same[1], other, table))
    rows = jnp.where(upper == 0, jnp.stack([mine, other]), jnp.stack([other, mine]))
    rows = spread(rows.reshape(n_zh * held * tile, width), "x")
    same.append(hop(same[1]))
    cross.append(hop(cross[1]))
    same[2], rows = lax.optimization_barrier((same[2], rows))
    rows = rows.reshape(-1, tile, width)
    n_y = n_yh * n_yl
    up = [(n, (n + 1) % n_y) for n in range(n_y)]
    down = [(n, (n - 1) % n_y) for n in range(n_y)]
    below, above = [rows], [rows]

    def pass_on():
        if len(below) < n_y // 2:
            below.append(lax.ppermute(below[-1], Y, up))
            above.append(lax.ppermute(above[-1], Y, down))
        else:
            cut = below[-1].shape[0] // 2
            below.append(lax.ppermute(below[-1][:cut], Y, up))
            above.append(lax.ppermute(above[-1][cut:], Y, down))

    pass_on()
    for step in range(2, ring // 2):
        if step == ring // 2 - 1:
            same[-1], below[1], above[1] = lax.optimization_barrier((same[-1], below[1], above[1]))
        same.append(hop(same[-1]))
        if step < ring // 2 - 1:
            cross.append(hop(cross[-1]))
    same[-1], cross[-1] = lax.optimization_barrier((same[-1], cross[-1]))
    pass_on()
    same[-1], below[2], above[2] = lax.optimization_barrier((same[-1], below[2], above[2]))
    far_twin = lax.ppermute(same[-1], "c", swap)
    pass_on()
    pass_on()

    blocks = same + cross[1:]
    near, far = n_x, n_zh * n_y
    sizes = (near, far * held, tile, share)
    send = gram(table, twin, far_twin, blocks, *sizes)
    received = lax.ppermute(send, "c", swap)
    terms = gram(table, own, same[-1], blocks, *sizes) + received
    terms = lax.all_to_all(terms, "x", 0, 0)
    terms = functools.reduce(jnp.add, [terms[n] for n in range(near)])
    terms, below[-1], above[-1] = lax.optimization_barrier((terms, below[-1], above[-1]))
    terms = lax.all_to_all(terms.reshape(far, -1, terms.shape[1]), ("zh",) + Y, 0, 0)
    terms = terms.reshape((n_zh, n_y) + terms.shape[1:])
    factor_tiles = sum_join(terms, held, tile, cols, 1.0 / (tokens * owners))

    owner, slot = assignment // held, assignment % held
    down_by = (lax.axis_index(Y) - owner) % n_y
    place_of = (down_by * n_x + owner // n_y % n_x) * n_zh + owner // (n_y * n_x)
    preconditioned = place(
        (place_of * held + slot).astype(jnp.int32), below + above[:0:-1]
    )
    return factor_tiles, preconditioned


def solution(mesh):
    split = Mesh(mesh.devices.reshape(2, 4, 4, 2, 4, 2), DP + GROUP)
    placed = (P(DP, GROUP), P(), P(DP, None, None), P(None, GROUP))
    return jax.shard_map(
        body,
        mesh=split,
        in_specs=placed,
        out_specs=(P(DP, None, GROUP), P(None, GROUP)),
        check_vma=False,
    )
```

```python
import functools

import jax
import jax.numpy as jnp
from jax import lax
from jax.experimental import pallas as pl
from jax.experimental.pallas import tpu as pltpu
from jax.sharding import Mesh, PartitionSpec as P

DP = ("zh", "x", "yh", "yl")
GROUP = ("zl", "c")
Y = ("yh", "yl")


def gram_kernel(table, slots, near_ref, far_ref, *refs):
    *blocks, out_ref, total = refs
    cols = near_ref.shape[0]
    share = total.shape[1]
    dest = pl.program_id(0)
    pairs = slots // 2
    high = out_ref.shape[1] // pairs
    tile = (high - 8) // 2
    count = pl.num_programs(0) * slots

    @pl.when(dest == 0)
    def _():
        mine = pl.ds(pl.multiple_of(table[count], 16), share)
        total[...] = jnp.zeros_like(total)
        for n, block in enumerate(blocks):
            at = pl.ds(pl.multiple_of(table[count + 1 + 2 * n], 8), cols)
            near = table[count + 2 + 2 * n] == 0
            factor = jnp.where(near, near_ref[mine, :], far_ref[mine, :])
            total[at, :] += lax.dot_general(
                block[...], factor, (((1,), (1,)), ((), ())), preferred_element_type=jnp.float32
            )

    for pair in range(pairs):
        both = []
        for n in range(2):
            t = table[dest * slots + 2 * pair + n]
            rows = total[pl.ds(pl.multiple_of(jnp.maximum(t, 0) * tile, 8), tile), :]
            both.append(jnp.where(t >= 0, rows, 0.0))
        out_ref[0, high * pair : high * (pair + 1), :] = pack(jnp.concatenate(both))


def pack(rows):
    n, cols = rows.shape
    rest = [rows[8 * k : 8 * k + 8, 128:] for k in range(n // 8)]
    rest.append(jnp.zeros((8, 128 - (cols - 128) * (n // 8)), rows.dtype))
    return jnp.concatenate([rows[:, :128], jnp.concatenate(rest, axis=1)])


def gram(table, near, far, blocks, dests, slots, tile, share):
    cols, tokens = near.shape
    high = 2 * tile + 8
    out = jax.ShapeDtypeStruct((dests, slots // 2 * high, 128), jnp.float32)
    given = [near, far, *blocks]
    return pl.pallas_call(
        lambda table_ref, *refs: gram_kernel(table_ref, slots, *refs),
        grid_spec=pltpu.PrefetchScalarGridSpec(
            num_scalar_prefetch=1,
            grid=(dests,),
            in_specs=[pl.BlockSpec((cols, tokens), lambda d, t: (0, 0))] * len(given),
            out_specs=pl.BlockSpec((1,) + out.shape[1:], lambda d, t: (d, 0, 0)),
            scratch_shapes=[pltpu.VMEM((len(blocks) * cols, share), jnp.float32)],
        ),
        out_shape=out,
        compiler_params=pltpu.CompilerParams(vmem_limit_bytes=24 * 2**20),
    )(table, *given)


def sum_join_kernel(scale, parts_ref, out_ref):
    held, tile, cols = out_ref.shape
    halves, rows = parts_ref.shape[1], held * tile
    extra = cols // halves - 128
    pieces = []
    for half in range(halves):
        total = parts_ref[0, half]
        for n in range(1, parts_ref.shape[0]):
            total = total + parts_ref[n, half]
        total = total * scale
        pieces.append(total[:rows])
        rest = total[rows:]
        pieces.append(
            jnp.concatenate([rest[:, extra * n : extra * (n + 1)] for n in range(rows // 8)])
        )
    joined = jnp.concatenate(pieces, axis=1)
    for slot in range(held):
        out_ref[slot] = joined[tile * slot : tile * (slot + 1)]


def sum_join(parts, held, tile, cols, scale):
    return pl.pallas_call(
        functools.partial(sum_join_kernel, scale),
        out_shape=jax.ShapeDtypeStruct((held, tile, cols), jnp.float32),
    )(parts)


def place_kernel(place_of, *refs):
    *blocks, out_ref, rows_ref = refs
    tile = rows_ref.shape[1]
    at = 0
    for block in blocks:
        rows_ref[at : at + block.shape[0]] = block[...]
        at += block.shape[0]
    for pair in range(out_ref.shape[0] // (2 * tile)):
        both = [rows_ref[place_of[2 * pair + n]].astype(jnp.float32) for n in range(2)]
        out_ref[2 * tile * pair : 2 * tile * (pair + 1), :] = jnp.concatenate(both).astype(
            out_ref.dtype
        )


def place(place_of, blocks):
    _, tile, cols = blocks[0].shape
    slots = sum(block.shape[0] for block in blocks)
    tiles = place_of.shape[0]
    return pl.pallas_call(
        place_kernel,
        grid_spec=pltpu.PrefetchScalarGridSpec(
            num_scalar_prefetch=1,
            grid=(1,),
            in_specs=[pl.BlockSpec(block.shape, lambda i, s: (0, 0, 0)) for block in blocks],
            out_specs=pl.BlockSpec((tiles * tile, cols), lambda i, s: (0, 0)),
            scratch_shapes=[pltpu.VMEM((slots, tile, cols), blocks[0].dtype)],
        ),
        out_shape=jax.ShapeDtypeStruct((tiles * tile, cols), blocks[0].dtype),
        compiler_params=pltpu.CompilerParams(vmem_limit_bytes=20 * 2**20),
    )(place_of, *blocks)


def spread(rows, axis):
    copies = jnp.broadcast_to(rows[None], (lax.axis_size(axis),) + rows.shape)
    return lax.all_to_all(copies, axis, 0, 0)


def body(sampled, assignment, inverse_rows, gradient):
    n_zh, n_x, n_yh, n_yl = (lax.axis_size(name) for name in DP)
    held, tile, order = inverse_rows.shape
    tiles = assignment.shape[0]
    tokens, cols = sampled.shape
    width = gradient.shape[1]
    owners = n_zh * n_x * n_yh * n_yl

    ring = n_zh * lax.axis_size("zl")
    hops = [(2 * r, 2 * ((r + 1) % ring)) for r in range(ring)]
    hops += [(2 * r + 1, 2 * ((r - 1) % ring) + 1) for r in range(ring)]
    swap = [(0, 1), (1, 0)]

    def hop(block):
        return lax.ppermute(block, ("zh", "zl", "c"), hops)

    owner_slots = owners * held
    index = jnp.arange(tiles, dtype=jnp.int32)
    table = jnp.full((owner_slots,), -1, jnp.int32).at[assignment].set(index)
    table = table.reshape(n_zh, n_x, n_yh, n_yl, held).transpose(1, 2, 3, 0, 4).reshape(-1)
    core, upper = lax.axis_index("c"), lax.axis_index("zh")
    here = upper * (ring // n_zh) + lax.axis_index("zl")
    share = cols // n_zh
    more = [upper * share]
    for steps, side in [(n, core) for n in range(ring // 2 + 1)] + [
        (n, 1 - core) for n in range(1, ring // 2)
    ]:
        chip = (here + jnp.where(core == 0, ring - steps, steps)) % ring
        row = (chip % (ring // n_zh) * 2 + side) * cols
        more += [row, (chip // (ring // n_zh) != upper).astype(jnp.int32)]
    table = jnp.concatenate([table, jnp.stack(more).astype(jnp.int32)])

    own = sampled.T
    twin = lax.ppermute(own, "c", swap)
    same, cross = [own, hop(own)], [twin, hop(twin)]

    inverse_rows, twin = lax.optimization_barrier((inverse_rows, twin))
    mine = jnp.dot(
        inverse_rows.reshape(held * tile, order), gradient, preferred_element_type=jnp.float32
    ).astype(jnp.bfloat16)
    other = lax.ppermute(mine, "zh", swap)
    same[1], other, table = lax.optimization_barrier((same[1], other, table))
    rows = jnp.where(upper == 0, jnp.stack([mine, other]), jnp.stack([other, mine]))
    rows = spread(rows.reshape(n_zh * held * tile, width), "x")
    same.append(hop(same[1]))
    cross.append(hop(cross[1]))
    same[2], rows = lax.optimization_barrier((same[2], rows))
    rows = rows.reshape(-1, tile, width)
    n_y = n_yh * n_yl
    up = [(n, (n + 1) % n_y) for n in range(n_y)]
    down = [(n, (n - 1) % n_y) for n in range(n_y)]
    below, above = [rows], [rows]

    def pass_on():
        below.append(lax.ppermute(below[-1], Y, up))
        if len(below) <= n_y // 2:
            above.append(lax.ppermute(above[-1], Y, down))

    pass_on()
    for step in range(2, ring // 2):
        if step == ring // 2 - 1:
            same[-1], below[1], above[1] = lax.optimization_barrier((same[-1], below[1], above[1]))
        same.append(hop(same[-1]))
        if step < ring // 2 - 1:
            cross.append(hop(cross[-1]))
    same[-1], cross[-1] = lax.optimization_barrier((same[-1], cross[-1]))
    pass_on()
    same[-1], below[2], above[2] = lax.optimization_barrier((same[-1], below[2], above[2]))
    far_twin = lax.ppermute(same[-1], "c", swap)
    pass_on()
    pass_on()

    blocks = same + cross[1:]
    near, far = n_x, n_zh * n_y
    sizes = (near, far * held, tile, share)
    send = gram(table, twin, far_twin, blocks, *sizes)
    received = lax.ppermute(send, "c", swap)
    terms = gram(table, own, same[-1], blocks, *sizes) + received
    terms = lax.all_to_all(terms, "x", 0, 0)
    terms = functools.reduce(jnp.add, [terms[n] for n in range(near)])
    terms, below[-1], above[-1] = lax.optimization_barrier((terms, below[-1], above[-1]))
    terms = lax.all_to_all(terms.reshape(far, -1, terms.shape[1]), Y + ("zh",), 0, 0)
    terms = terms.reshape((n_y, n_zh) + terms.shape[1:])
    factor_tiles = sum_join(terms, held, tile, cols, 1.0 / (tokens * owners))

    owner, slot = assignment // held, assignment % held
    down_by = (lax.axis_index(Y) - owner) % n_y
    place_of = (down_by * n_x + owner // n_y % n_x) * n_zh + owner // (n_y * n_x)
    preconditioned = place(
        (place_of * held + slot).astype(jnp.int32), below + above[:0:-1]
    )
    return factor_tiles, preconditioned


def solution(mesh):
    split = Mesh(mesh.devices.reshape(2, 4, 4, 2, 4, 2), DP + GROUP)
    placed = (P(DP, GROUP), P(), P(DP, None, None), P(None, GROUP))
    return jax.shard_map(
        body,
        mesh=split,
        in_specs=placed,
        out_specs=(P(DP, None, GROUP), P(None, GROUP)),
        check_vma=False,
    )
```
